32 devices in a mesh: dp: 16 (over z, y, x), head: 2 (over core).
Axes of the slice: x: 2, y: 2, z: 4, core: 2. Of those that a mesh axis runs over, the one named last changes fastest.
Arguments:
- queries: bfloat16 [2048, 12288], P('dp', 'head'), may hold values from -128 to 128
- keys: bfloat16 [2048, 1024], P('dp', 'head'), may hold values from -6 to 6
- values: bfloat16 [2048, 1024], P('dp', 'head'), may hold values from -6 to 6
- grad_out: bfloat16 [2048, 12288], P(('dp', 'head')), may hold values from -6 to 6
- segments: int32 [2048], replicated, may hold values from 0 to 3, never falling along the last dimension, each value on 1 to 1024 neighbouring positions
Outputs:
- attention_out: bfloat16 [2048, 12288], P(('dp', 'head'))
- grad_queries: bfloat16 [2048, 12288], P('dp', 'head')
- grad_keys: bfloat16 [2048, 1024], P('dp', 'head')
- grad_values: bfloat16 [2048, 1024], P('dp', 'head')
The draws below stay inside these ranges and needn't reach their ends.
Inputs may be any that keep to these rules, and one draw needn't show every extreme that they name: segments never fall; each document holds 1 to 1024 tokens and one holds exactly 1024.
All inputs are finite; a program needn't handle non-finite values.
Results may differ from the reference program's by a relative error of at most 0.011.
Values may be sent and summed in bfloat16 or wider, within the bound.
A program may use at most 128 MiB of HBM per device.

```python
import math
import jax
import jax.numpy as jnp
import numpy as np
from jax import lax

QHEADS = 96
KVHEADS = 8
HEAD_DIM = 128
ROWS = 128
DEPTH = 8
MAXDOC = 1024
TOKENS = 2048
DOCS = 4


def shared_draw(key):
    base_keys = jnp.clip(jax.random.normal(jax.random.fold_in(key, 13), (TOKENS, KVHEADS * HEAD_DIM), jnp.float32), -6.0, 6.0)
    return base_keys


def draw_keys(key, part):
    base_keys = shared_draw(key)
    result = base_keys
    return result.astype(jnp.bfloat16)


def draw_queries(key, part):
    key = jax.random.fold_in(key, 5)
    result = jnp.clip(jax.random.normal(key, (TOKENS, QHEADS * HEAD_DIM), jnp.float32), -6.0, 6.0)
    return result.astype(jnp.bfloat16)


def block_scale(key, shape, pieces, least, high):
    gain = 1.0
    for dim, blocks in pieces:
        heights = jax.random.uniform(jax.random.fold_in(jax.random.fold_in(key, 6), dim), (blocks,), jnp.float32, least / len(pieces), high / len(pieces))
        gain = gain * jnp.repeat(jnp.exp(heights), shape[dim] // blocks).reshape((-1,) + (1,) * (len(shape) - 1 - dim))
    return gain


def split_up(count, total, reach, slope):
    portions = [(1 << 20) // math.isqrt(rank ** slope) + 1 for rank in range(2, count + 1)]
    surplus, counts = total - reach - (count - 1), [1] * (count - 1)
    while surplus > 0:
        movable = [i for i in range(count - 1) if counts[i] < reach]
        whole, remaining = sum([portions[i] for i in movable]), surplus
        for i in movable:
            extra = min(reach - counts[i], max(1, remaining * portions[i] // whole), surplus)
            counts[i] = counts[i] + extra
            surplus = surplus - extra
    return np.array([reach] + counts)


def uneven_parts(own_key, number_of, total, bound, lean):
    if number_of == 2:
        one = jax.random.randint(own_key, (), max(1, total - bound), min(bound, total - 1) + 1)
        return jnp.stack([one, total - one])
    sizes = jnp.asarray(split_up(number_of, total, bound, lean), jnp.int32)
    twos = (number_of - 1) // 2
    giver, taker = sizes[1:1 + 2 * twos:2], sizes[2:2 + 2 * twos:2]
    slack = jnp.minimum(giver - 1, bound - taker)
    shifted = jax.random.randint(jax.random.fold_in(own_key, 1), (twos,), 0, 1 << 20) % (slack + 1)
    sizes = sizes.at[1:1 + 2 * twos:2].set(giver - shifted).at[2:2 + 2 * twos:2].set(taker + shifted)
    return sizes[jax.random.permutation(jax.random.fold_in(own_key, 2), number_of)]


def gaussian(rng, shape, spread, most, shards=(), kind=jnp.bfloat16):
    drawn = jax.random.normal(rng, shape, jnp.float32) * spread
    if len(shards) > 0:
        drawn = block_scale(rng, shape, shards, -0.22, 0.18) * drawn
    return jnp.clip(drawn, min=-most, max=most).astype(kind)


def setup_inputs(seed: int = 0) -> dict:
    splits = jax.random.split(jax.random.key(seed), 6)
    return {
        "queries": draw_queries(jax.random.fold_in(splits[5], 71), 0),
        "keys": draw_keys(jax.random.fold_in(splits[5], 71), 0),
        "values": gaussian(splits[2], (TOKENS, KVHEADS * HEAD_DIM), 1.0, 6.0, ((0, 16), (1, 2))),
        "grad_out": gaussian(splits[3], (TOKENS, QHEADS * HEAD_DIM), 1.0, 6.0, ((0, 32),)),
        "segments": jnp.searchsorted(jnp.cumsum(uneven_parts(splits[4], DOCS, TOKENS, MAXDOC, 2)), jnp.arange(TOKENS), side="right").astype(jnp.int32),
    }


def block_terms(query_rows, cotangent_rows, key_window, value_window, allowed):
    group_size = QHEADS // KVHEADS
    row_count = query_rows.shape[0]
    window = key_window.shape[0]
    softmax_scale = 1.0 / math.sqrt(HEAD_DIM)
    query_heads = query_rows.astype(jnp.float32).reshape(row_count, KVHEADS, group_size, HEAD_DIM)
    cotangent_heads = cotangent_rows.astype(jnp.float32).reshape(row_count, KVHEADS, group_size, HEAD_DIM)
    key_heads = key_window.astype(jnp.float32).reshape(window, KVHEADS, HEAD_DIM)
    value_heads = value_window.astype(jnp.float32).reshape(window, KVHEADS, HEAD_DIM)
    products = jnp.einsum('rkgd,wkd->kgrw', query_heads, key_heads)
    scores = jnp.where(allowed, softmax_scale * products, -jnp.inf)
    row_max = lax.optimization_barrier(jnp.max(scores, axis=-1, keepdims=True))
    exp_total = lax.optimization_barrier(jnp.sum(jnp.exp(scores - row_max), axis=-1, keepdims=True))
    log_total = row_max + jnp.log(exp_total)
    weights = jnp.exp(scores - log_total)
    weights_low = lax.optimization_barrier(weights.astype(jnp.bfloat16)).astype(jnp.float32)
    out_heads = jnp.einsum('kgrw,wkd->rkgd', weights_low, value_heads)
    out_low = lax.optimization_barrier(out_heads.astype(jnp.bfloat16))
    row_delta = lax.optimization_barrier(jnp.sum(cotangent_heads * out_low.astype(jnp.float32), axis=-1))
    grad_weights = jnp.einsum('rkgd,wkd->kgrw', cotangent_heads, value_heads)
    grad_scores = weights * (grad_weights - jnp.transpose(row_delta, (1, 2, 0))[..., None])
    grad_low = lax.optimization_barrier(grad_scores.astype(jnp.bfloat16)).astype(jnp.float32)
    grad_query = (softmax_scale * jnp.einsum('kgrw,wkd->rkgd', grad_low, key_heads)).astype(jnp.bfloat16)
    grad_key = softmax_scale * jnp.einsum('kgrw,rkgd->wkd', grad_low, query_heads)
    grad_value = jnp.einsum('kgrw,rkgd->wkd', weights_low, cotangent_heads)
    return (out_low.reshape(row_count, -1), grad_query.reshape(row_count, -1), grad_key.reshape(window, -1), grad_value.reshape(window, -1))

def reference(queries, keys, values, grad_out, segments):
    padding = DEPTH * ROWS
    window = (DEPTH + 1) * ROWS
    width = KVHEADS * HEAD_DIM
    doc_ids = segments.astype(jnp.int32)
    key_pad = jnp.concatenate([jnp.zeros((padding, width), keys.dtype), keys], axis=0)
    value_pad = jnp.concatenate([jnp.zeros((padding, width), values.dtype), values], axis=0)
    seg_pad = jnp.concatenate([jnp.full((padding,), -1, jnp.int32), doc_ids])

    def step(carry, block_index):
        key_sum, value_sum = carry
        first_row = (block_index * ROWS).astype(jnp.int32)
        query_rows = lax.dynamic_slice_in_dim(queries, first_row, ROWS, 0)
        cotangent_rows = lax.dynamic_slice_in_dim(grad_out, first_row, ROWS, 0)
        key_window = lax.dynamic_slice_in_dim(key_pad, first_row, window, 0)
        value_window = lax.dynamic_slice_in_dim(value_pad, first_row, window, 0)
        seg_query = lax.dynamic_slice_in_dim(doc_ids, first_row, ROWS, 0)
        seg_keys = lax.dynamic_slice_in_dim(seg_pad, first_row, window, 0)
        query_pos = first_row + jnp.arange(ROWS, dtype=jnp.int32)
        key_pos = first_row - padding + jnp.arange(window, dtype=jnp.int32)
        allowed = (seg_query[:, None] == seg_keys[None, :]) & (key_pos[None, :] <= query_pos[:, None])
        out_rows, dq_rows, dk_window, dv_window = block_terms(query_rows, cotangent_rows, key_window, value_window, allowed)
        key_old = lax.dynamic_slice_in_dim(key_sum, first_row, window, 0)
        key_sum = lax.dynamic_update_slice_in_dim(key_sum, key_old + dk_window, first_row, 0)
        value_old = lax.dynamic_slice_in_dim(value_sum, first_row, window, 0)
        value_sum = lax.dynamic_update_slice_in_dim(value_sum, value_old + dv_window, first_row, 0)
        return ((key_sum, value_sum), (out_rows, dq_rows))
    start_sums = (jnp.zeros((padding + TOKENS, width), jnp.float32), jnp.zeros((padding + TOKENS, width), jnp.float32))
    (key_sum, value_sum), (out_blocks, dq_blocks) = lax.scan(step, start_sums, jnp.arange(TOKENS // ROWS, dtype=jnp.int32))
    attention_out = out_blocks.reshape(TOKENS, QHEADS * HEAD_DIM)
    grad_queries = dq_blocks.reshape(TOKENS, QHEADS * HEAD_DIM)
    return (attention_out, grad_queries, key_sum[padding:].astype(jnp.bfloat16), value_sum[padding:].astype(jnp.bfloat16))
```

```python
import functools
import math

import jax
import jax.numpy as jnp
from jax import lax
from jax.experimental import pallas as pl
from jax.experimental.pallas import tpu as pltpu
from jax.sharding import PartitionSpec as P

QHEADS = 96
KVHEADS = 8
HEAD_DIM = 128
DEPTH = 8
SPAN = DEPTH + 1
GROUP = QHEADS // KVHEADS
PAIRS = GROUP // 2
MASKED = -(2.0**100)
SCALE = 1.0 / math.sqrt(HEAD_DIM)
NT = (((1,), (1,)), ((), ()))


def dot(a, b):
    return jnp.dot(a, b, preferred_element_type=jnp.float32)


def dot_nt(a, b):
    return lax.dot_general(a, b, NT, preferred_element_type=jnp.float32)


def attend_group(q_at, g_at, k_at, v_at, put_out, put_dq, put_dk, put_dv, tmp):
    (k_aug, v_aug, k_t, v_t, q_aug, g_aug, q_norm, g_norm, score, p_all, ds_all) = tmp
    rows = HEAD_DIM
    for j in range(SPAN):
        at = pl.ds(j * rows, rows)
        k_j, v_j = k_at(j), v_at(j)
        k_aug[at, :HEAD_DIM] = k_j
        v_aug[at, :HEAD_DIM] = v_j
        k_t[:, j * rows : (j + 1) * rows] = k_j.T
        v_t[:, j * rows : (j + 1) * rows] = v_j.T
    for h in range(GROUP):
        q_aug[h * rows : (h + 1) * rows, :HEAD_DIM] = q_at(h)
        g_aug[h * rows : (h + 1) * rows, :HEAD_DIM] = g_at(h)

    two = 2 * rows
    lane = lax.broadcasted_iota(jnp.int32, (two, HEAD_DIM), 1)

    def pair_step(pair, carry):
        cols = pl.ds(pl.multiple_of(pair * two, two), two)
        q_pair = q_aug[cols, :]
        score[...] = dot_nt(k_aug[...], q_pair)
        top = score[0:rows, :].reshape(rows // 8, 8, two).max(axis=0)
        for j in range(1, SPAN):
            part = score[j * rows : (j + 1) * rows, :]
            top = jnp.maximum(top, part.reshape(rows // 8, 8, two).max(axis=0))
        top = jnp.max(top, axis=0, keepdims=True)
        total = jnp.zeros((8, two), jnp.float32)
        for j in range(SPAN):
            part = score[j * rows : (j + 1) * rows, :]
            e = jnp.exp2((part - top) * (SCALE * math.log2(math.e)))
            total = total + e.reshape(rows // 8, 8, two).sum(axis=0)
            p_all[j * rows : (j + 1) * rows, cols] = e.astype(jnp.bfloat16)
        inv = 1.0 / jnp.sum(total, axis=0, keepdims=True)
        inv_t = jnp.broadcast_to(inv, (HEAD_DIM, two)).T
        p = p_all[:, cols]
        out = (dot(v_t[...], p).T * inv_t).astype(jnp.bfloat16)
        put_out(2 * pair, out[:rows])
        put_out(2 * pair + 1, out[rows:])
        g_pair = g_aug[cols, :HEAD_DIM].astype(jnp.float32)
        delta = -jnp.sum(g_pair * out.astype(jnp.float32), axis=1, keepdims=True)
        hi = delta.astype(jnp.bfloat16).astype(jnp.float32)
        mid = (delta - hi).astype(jnp.bfloat16).astype(jnp.float32)
        low = delta - hi - mid
        tail = jnp.where(lane == 0, hi, jnp.where(lane == 1, mid, jnp.where(lane == 2, low, 0.0)))
        g_aug[cols, HEAD_DIM:] = tail.astype(jnp.bfloat16)
        q_norm[cols, :] = (q_pair[:, :HEAD_DIM].astype(jnp.float32) * inv_t).astype(jnp.bfloat16)
        g_norm[cols, :] = (g_pair * inv_t).astype(jnp.bfloat16)
        score[...] = dot_nt(v_aug[...], g_aug[cols, :])
        for j in range(SPAN):
            at = slice(j * rows, (j + 1) * rows)
            ds_all[at, cols] = (p_all[at, cols].astype(jnp.float32) * score[at, :]).astype(jnp.bfloat16)
        dq = (dot(k_t[...], ds_all[:, cols]).T * (inv_t * SCALE)).astype(jnp.bfloat16)
        put_dq(2 * pair, dq[:rows])
        put_dq(2 * pair + 1, dq[rows:])
        return carry

    lax.fori_loop(0, PAIRS, pair_step, 0)
    for j in range(SPAN):
        at = slice(j * rows, (j + 1) * rows)
        put_dk(j, (SCALE * dot(ds_all[at, :], q_norm[...])).astype(jnp.bfloat16))
        put_dv(j, dot(p_all[at, :], g_norm[...]).astype(jnp.bfloat16))


def fill_constants(mask_ref, tmp):
    k_aug, v_aug, q_aug = tmp[0], tmp[1], tmp[4]
    k_aug[:, HEAD_DIM:] = mask_ref[...]
    ones = lax.broadcasted_iota(jnp.int32, (v_aug.shape[0], HEAD_DIM), 1) < 3
    v_aug[:, HEAD_DIM:] = jnp.where(ones, 1.0, 0.0).astype(jnp.bfloat16)
    side = (q_aug.shape[0], HEAD_DIM)
    row = lax.broadcasted_iota(jnp.int32, side, 0) % HEAD_DIM
    eye = row == lax.broadcasted_iota(jnp.int32, side, 1)
    q_aug[:, HEAD_DIM:] = jnp.where(eye, 1.0, 0.0).astype(jnp.bfloat16)


def scratch(rows):
    window, queries = SPAN * rows, GROUP * rows
    return [
        pltpu.VMEM((window, 2 * HEAD_DIM), jnp.bfloat16),
        pltpu.VMEM((window, 2 * HEAD_DIM), jnp.bfloat16),
        pltpu.VMEM((HEAD_DIM, window), jnp.bfloat16),
        pltpu.VMEM((HEAD_DIM, window), jnp.bfloat16),
        pltpu.VMEM((queries, 2 * HEAD_DIM), jnp.bfloat16),
        pltpu.VMEM((queries, 2 * HEAD_DIM), jnp.bfloat16),
        pltpu.VMEM((queries, HEAD_DIM), jnp.bfloat16),
        pltpu.VMEM((queries, HEAD_DIM), jnp.bfloat16),
        pltpu.VMEM((window, 2 * rows), jnp.float32),
        pltpu.VMEM((window, queries), jnp.bfloat16),
        pltpu.VMEM((window, queries), jnp.bfloat16),
    ]


def kernel(q_ref, g_ref, kv_ref, mask_ref, out_ref, dq_ref, dkv_ref, *tmp):
    @pl.when(pl.program_id(0) == 0)
    def _():
        fill_constants(mask_ref, tmp)

    def at(ref, h):
        return ref[:, h * HEAD_DIM : (h + 1) * HEAD_DIM]

    def put(ref, h, value):
        ref[:, pl.ds(pl.multiple_of(h * HEAD_DIM, HEAD_DIM), HEAD_DIM)] = value

    def put_block(which, j, value):
        dkv_ref[j, 0, which] = value

    attend_group(
        functools.partial(at, q_ref),
        functools.partial(at, g_ref),
        lambda j: kv_ref[j, 0, 0],
        lambda j: kv_ref[j, 0, 1],
        functools.partial(put, out_ref),
        functools.partial(put, dq_ref),
        functools.partial(put_block, 0),
        functools.partial(put_block, 1),
        tmp,
    )


def attention(queries, grad_heads, kv_window, mask):
    rows, columns = queries.shape
    heads = columns // (GROUP * HEAD_DIM)
    head_spec = pl.BlockSpec((rows, GROUP * HEAD_DIM), lambda h: (0, h))
    kv_spec = pl.BlockSpec((SPAN, 1, 2, rows, HEAD_DIM), lambda h: (0, h, 0, 0, 0))
    return pl.pallas_call(
        kernel,
        grid=(heads,),
        in_specs=[head_spec, head_spec, kv_spec, pl.BlockSpec(mask.shape, lambda h: (0, 0))],
        out_specs=[head_spec, head_spec, kv_spec],
        out_shape=[
            jax.ShapeDtypeStruct(queries.shape, jnp.bfloat16),
            jax.ShapeDtypeStruct(queries.shape, jnp.bfloat16),
            jax.ShapeDtypeStruct(kv_window.shape, jnp.bfloat16),
        ],
        scratch_shapes=scratch(rows),
        compiler_params=pltpu.CompilerParams(vmem_limit_bytes=48 * 1024 * 1024),
        name="attention",
    )(queries, grad_heads, kv_window, mask)


def window_mask(segments, index, rows):
    padding = DEPTH * rows
    base = index * rows
    seg_pad = jnp.concatenate([jnp.full((padding,), -1, jnp.int32), segments])
    seg_query = lax.dynamic_slice_in_dim(segments, base, rows, 0)
    seg_keys = lax.dynamic_slice_in_dim(seg_pad, base, SPAN * rows, 0)
    query_pos = jnp.arange(rows, dtype=jnp.int32)
    key_pos = jnp.arange(SPAN * rows, dtype=jnp.int32) - padding
    allowed = (seg_keys[:, None] == seg_query[None, :]) & (key_pos[:, None] <= query_pos[None, :])
    return jnp.where(allowed, 0.0, MASKED).astype(jnp.bfloat16)


def shift(value, steps):
    count = lax.axis_size("dp")
    first, last = max(0, -steps), min(count, count - steps)
    return lax.ppermute(value, "dp", [(s, s + steps) for s in range(first, last)])


def body(queries, keys, values, grad_out, segments):
    rows = queries.shape[0]
    heads = keys.shape[1] // HEAD_DIM
    index = lax.axis_index("dp")
    mask = window_mask(segments, index, rows)
    kv = jnp.stack([keys.reshape(rows, heads, HEAD_DIM), values.reshape(rows, heads, HEAD_DIM)])
    kv = kv.transpose(2, 0, 1, 3)
    parts = [shift(kv, distance) for distance in range(DEPTH, 0, -1)] + [kv]
    kv_window = jnp.stack(parts)
    grad_heads = lax.all_to_all(grad_out, "head", split_axis=1, concat_axis=0, tiled=True)
    out, grad_queries, dkv = attention(queries, grad_heads, kv_window, mask)
    total = dkv[DEPTH].astype(jnp.float32)
    for distance in range(1, SPAN):
        total = total + shift(dkv[DEPTH - distance], -distance).astype(jnp.float32)
    total = total.astype(jnp.bfloat16).transpose(1, 2, 0, 3).reshape(2, rows, heads * HEAD_DIM)
    attention_out = lax.all_to_all(out, "head", split_axis=0, concat_axis=1, tiled=True)
    return attention_out, grad_queries, total[0], total[1]


def solution(mesh):
    placed = (P("dp", "head"), P("dp", "head"), P("dp", "head"), P(("dp", "head"), None), P())
    return jax.shard_map(
        body,
        mesh=mesh,
        in_specs=placed,
        out_specs=(P(("dp", "head"), None), P("dp", "head"), P("dp", "head"), P("dp", "head")),
        check_vma=False,
    )
```

```python
import functools
import math

import jax
import jax.numpy as jnp
from jax import lax
from jax.experimental import pallas as pl
from jax.experimental.pallas import tpu as pltpu
from jax.sharding import PartitionSpec as P

QHEADS = 96
KVHEADS = 8
HEAD_DIM = 128
DEPTH = 8
SPAN = DEPTH + 1
GROUP = QHEADS // KVHEADS
PAIRS = GROUP // 2
MASKED = -(2.0**100)
SCALE = 1.0 / math.sqrt(HEAD_DIM)
NT = (((1,), (1,)), ((), ()))


def dot(a, b):
    return jnp.dot(a, b, preferred_element_type=jnp.float32)


def dot_nt(a, b):
    return lax.dot_general(a, b, NT, preferred_element_type=jnp.float32)


def attend_group(q_at, g_at, k_at, v_at, put_out, put_dq, put_dk, put_dv, tmp):
    (k_aug, v_aug, k_t, v_t, q_aug, g_aug, q_norm, g_norm, score, p_all, ds_all) = tmp
    rows = HEAD_DIM
    for j in range(SPAN):
        at = pl.ds(j * rows, rows)
        k_j, v_j = k_at(j), v_at(j)
        k_aug[at, :HEAD_DIM] = k_j
        v_aug[at, :HEAD_DIM] = v_j
        k_t[:, j * rows : (j + 1) * rows] = k_j.T
        v_t[:, j * rows : (j + 1) * rows] = v_j.T
    for h in range(GROUP):
        q_aug[h * rows : (h + 1) * rows, :HEAD_DIM] = q_at(h)
        g_aug[h * rows : (h + 1) * rows, :HEAD_DIM] = g_at(h)

    two = 2 * rows
    lane = lax.broadcasted_iota(jnp.int32, (two, HEAD_DIM), 1)

    def pair_step(pair, carry):
        cols = pl.ds(pl.multiple_of(pair * two, two), two)
        q_pair = q_aug[cols, :]
        score[...] = dot_nt(k_aug[...], q_pair)
        top = score[0:rows, :].reshape(rows // 8, 8, two).max(axis=0)
        for j in range(1, SPAN):
            part = score[j * rows : (j + 1) * rows, :]
            top = jnp.maximum(top, part.reshape(rows // 8, 8, two).max(axis=0))
        top = jnp.max(top, axis=0, keepdims=True)
        total = jnp.zeros((8, two), jnp.float32)
        for j in range(SPAN):
            part = score[j * rows : (j + 1) * rows, :]
            e = jnp.exp2((part - top) * (SCALE * math.log2(math.e)))
            total = total + e.reshape(rows // 8, 8, two).sum(axis=0)
            p_all[j * rows : (j + 1) * rows, cols] = e.astype(jnp.bfloat16)
        inv = 1.0 / jnp.sum(total, axis=0, keepdims=True)
        inv_t = jnp.broadcast_to(inv, (HEAD_DIM, two)).T
        p = p_all[:, cols]
        out = (dot(v_t[...], p).T * inv_t).astype(jnp.bfloat16)
        put_out(2 * pair, out[:rows])
        put_out(2 * pair + 1, out[rows:])
        g_pair = g_aug[cols, :HEAD_DIM].astype(jnp.float32)
        delta = -jnp.sum(g_pair * out.astype(jnp.float32), axis=1, keepdims=True)
        hi = delta.astype(jnp.bfloat16).astype(jnp.float32)
        mid = (delta - hi).astype(jnp.bfloat16).astype(jnp.float32)
        low = delta - hi - mid
        tail = jnp.where(lane == 0, hi, jnp.where(lane == 1, mid, jnp.where(lane == 2, low, 0.0)))
        g_aug[cols, HEAD_DIM:] = tail.astype(jnp.bfloat16)
        q_norm[cols, :] = (q_pair[:, :HEAD_DIM].astype(jnp.float32) * inv_t).astype(jnp.bfloat16)
        g_norm[cols, :] = (g_pair * inv_t).astype(jnp.bfloat16)
        score[...] = dot_nt(v_aug[...], g_aug[cols, :])
        for j in range(SPAN):
            at = slice(j * rows, (j + 1) * rows)
            ds_all[at, cols] = (p_all[at, cols].astype(jnp.float32) * score[at, :]).astype(jnp.bfloat16)
        dq = (dot(k_t[...], ds_all[:, cols]).T * (inv_t * SCALE)).astype(jnp.bfloat16)
        put_dq(2 * pair, dq[:rows])
        put_dq(2 * pair + 1, dq[rows:])
        return carry

    lax.fori_loop(0, PAIRS, pair_step, 0)
    for j in range(SPAN):
        at = slice(j * rows, (j + 1) * rows)
        put_dk(j, (SCALE * dot(ds_all[at, :], q_norm[...])).astype(jnp.bfloat16))
        put_dv(j, dot(p_all[at, :], g_norm[...]).astype(jnp.bfloat16))


def fill_constants(mask_ref, tmp):
    k_aug, v_aug, q_aug = tmp[0], tmp[1], tmp[4]
    k_aug[:, HEAD_DIM:] = mask_ref[...]
    ones = lax.broadcasted_iota(jnp.int32, (v_aug.shape[0], HEAD_DIM), 1) < 3
    v_aug[:, HEAD_DIM:] = jnp.where(ones, 1.0, 0.0).astype(jnp.bfloat16)
    side = (q_aug.shape[0], HEAD_DIM)
    row = lax.broadcasted_iota(jnp.int32, side, 0) % HEAD_DIM
    eye = row == lax.broadcasted_iota(jnp.int32, side, 1)
    q_aug[:, HEAD_DIM:] = jnp.where(eye, 1.0, 0.0).astype(jnp.bfloat16)


def scratch(rows):
    window, queries = SPAN * rows, GROUP * rows
    return [
        pltpu.VMEM((window, 2 * HEAD_DIM), jnp.bfloat16),
        pltpu.VMEM((window, 2 * HEAD_DIM), jnp.bfloat16),
        pltpu.VMEM((HEAD_DIM, window), jnp.bfloat16),
        pltpu.VMEM((HEAD_DIM, window), jnp.bfloat16),
        pltpu.VMEM((queries, 2 * HEAD_DIM), jnp.bfloat16),
        pltpu.VMEM((queries, 2 * HEAD_DIM), jnp.bfloat16),
        pltpu.VMEM((queries, HEAD_DIM), jnp.bfloat16),
        pltpu.VMEM((queries, HEAD_DIM), jnp.bfloat16),
        pltpu.VMEM((window, 2 * rows), jnp.float32),
        pltpu.VMEM((window, queries), jnp.bfloat16),
        pltpu.VMEM((window, queries), jnp.bfloat16),
    ]


MESH = pl.DeviceIdType.MESH


def kernel(count, q_ref, grad_ref, key_ref, value_ref, mask_ref, out_ref, dq_ref, dk_ref, dv_ref,
           window, partial, arrived, g_heads, o_heads, o_arrived,
           kv_send, kv_recv, part_send, part_recv, g_send, g_recv, o_send, o_recv, *tmp):
    me, core = lax.axis_index("dp"), lax.axis_index("head")
    heads = window.shape[0]
    half, columns = grad_ref.shape[0], q_ref.shape[1]
    width = GROUP * HEAD_DIM

    def lanes(start, size):
        return pl.ds(pl.multiple_of(start, HEAD_DIM), size)

    mine, other = core * columns, (1 - core) * columns
    my_rows = pl.ds(pl.multiple_of(core * half, half), half)
    other_rows = pl.ds(pl.multiple_of((1 - core) * half, half), half)

    def kv_copy(h, d):
        return pltpu.make_async_remote_copy(
            window.at[h, DEPTH], window.at[h, DEPTH - d], kv_send.at[h, d - 1], kv_recv.at[h, d - 1],
            device_id=(lax.rem(me + d, count), core), device_id_type=MESH)

    def part_copy(h, d):
        return pltpu.make_async_remote_copy(
            partial.at[h, DEPTH - d], arrived.at[h, d - 1], part_send.at[h, d - 1], part_recv.at[h, d - 1],
            device_id=(lax.rem(me - d + count, count), core), device_id_type=MESH)

    def g_copy(h):
        return pltpu.make_async_remote_copy(
            grad_ref.at[:, lanes(other + h * width, width)], g_heads.at[my_rows, lanes(h * width, width)],
            g_send.at[h], g_recv.at[h], device_id=(me, 1 - core), device_id_type=MESH)

    def o_copy(h):
        return pltpu.make_async_remote_copy(
            o_heads.at[other_rows, lanes(h * width, width)], o_arrived.at[:, lanes(h * width, width)],
            o_send.at[h], o_recv.at[h], device_id=(me, 1 - core), device_id_type=MESH)

    barrier = pltpu.get_barrier_semaphore()
    pl.semaphore_signal(barrier, inc=1, device_id=(me, 1 - core), device_id_type=MESH)
    for d in range(1, SPAN):
        @pl.when(me + d < count)
        def _():
            pl.semaphore_signal(barrier, inc=1, device_id=(lax.rem(me + d, count), core), device_id_type=MESH)

        @pl.when(me >= d)
        def _():
            pl.semaphore_signal(barrier, inc=1, device_id=(lax.rem(me - d + count, count), core), device_id_type=MESH)

    for h in range(heads):
        window[h, DEPTH, 0] = key_ref[:, h * HEAD_DIM : (h + 1) * HEAD_DIM]
        window[h, DEPTH, 1] = value_ref[:, h * HEAD_DIM : (h + 1) * HEAD_DIM]
    for d in range(1, SPAN):
        @pl.when(me < d)
        def _():
            window[:, DEPTH - d] = jnp.zeros((heads,) + window.shape[2:], jnp.bfloat16)

    pl.semaphore_wait(barrier, 1 + jnp.minimum(me, DEPTH) + jnp.minimum(count - 1 - me, DEPTH))

    def start_head(h, carry):
        g_copy(h).start()
        for d in range(1, SPAN):
            @pl.when(me + d < count)
            def _():
                kv_copy(h, d).start()
        return carry

    lax.fori_loop(0, heads, start_head, 0)
    g_heads[my_rows, :] = grad_ref[:, lanes(mine, columns)]
    fill_constants(mask_ref, tmp)

    def head_step(h, carry):
        g_copy(h).wait_recv()
        for d in range(1, SPAN):
            @pl.when(me >= d)
            def _():
                kv_copy(h, d).wait_recv()

        def at(ref, g):
            return ref[:, lanes(h * width + g * HEAD_DIM, HEAD_DIM)]

        def put(ref, g, value):
            ref[:, lanes(h * width + g * HEAD_DIM, HEAD_DIM)] = value

        def put_block(which, j, value):
            partial[h, j, which] = value

        attend_group(
            functools.partial(at, q_ref),
            functools.partial(at, g_heads),
            lambda j: window[h, j, 0],
            lambda j: window[h, j, 1],
            functools.partial(put, o_heads),
            functools.partial(put, dq_ref),
            functools.partial(put_block, 0),
            functools.partial(put_block, 1),
            tmp,
        )
        for d in range(1, SPAN):
            @pl.when(me >= d)
            def _():
                part_copy(h, d).start()
        o_copy(h).start()
        out_ref[:, lanes(mine + h * width, width)] = o_heads[my_rows, lanes(h * width, width)]
        return carry

    lax.fori_loop(0, heads, head_step, 0)

    def finish_head(h, carry):
        g_copy(h).wait_send()
        o_copy(h).wait()
        for d in range(1, SPAN):
            @pl.when(me + d < count)
            def _():
                kv_copy(h, d).wait_send()
                part_copy(h, d).wait_recv()

            @pl.when(me + d >= count)
            def _():
                arrived[h, d - 1] = jnp.zeros(arrived.shape[2:], jnp.bfloat16)

            @pl.when(me >= d)
            def _():
                part_copy(h, d).wait_send()

        total = partial[h, DEPTH].astype(jnp.float32)
        for d in range(1, SPAN):
            total = total + arrived[h, d - 1].astype(jnp.float32)
        dk_ref[:, lanes(h * HEAD_DIM, HEAD_DIM)] = total[0].astype(jnp.bfloat16)
        dv_ref[:, lanes(h * HEAD_DIM, HEAD_DIM)] = total[1].astype(jnp.bfloat16)
        return carry

    lax.fori_loop(0, heads, finish_head, 0)
    out_ref[:, lanes(other, columns)] = o_arrived[...]


def attention(count, queries, grad_out, keys, values, mask):
    rows, columns = queries.shape
    heads = keys.shape[1] // HEAD_DIM
    half = grad_out.shape[0]
    tile = (2, rows, HEAD_DIM)
    sems = pltpu.SemaphoreType.DMA
    in_vmem = pl.BlockSpec(memory_space=pltpu.VMEM)
    return pl.pallas_call(
        functools.partial(kernel, count),
        in_specs=[in_vmem] * 5,
        out_specs=[in_vmem] * 4,
        out_shape=[jax.ShapeDtypeStruct(a.shape, jnp.bfloat16) for a in (grad_out, queries, keys, values)],
        scratch_shapes=[
            pltpu.VMEM((heads, SPAN) + tile, jnp.bfloat16),
            pltpu.VMEM((heads, SPAN) + tile, jnp.bfloat16),
            pltpu.VMEM((heads, DEPTH) + tile, jnp.bfloat16),
            pltpu.VMEM((rows, columns), jnp.bfloat16),
            pltpu.VMEM((rows, columns), jnp.bfloat16),
            pltpu.VMEM((half, columns), jnp.bfloat16),
            sems((heads, DEPTH)), sems((heads, DEPTH)), sems((heads, DEPTH)), sems((heads, DEPTH)),
            sems((heads,)), sems((heads,)), sems((heads,)), sems((heads,)),
        ] + scratch(rows),
        compiler_params=pltpu.CompilerParams(
            vmem_limit_bytes=56 * 1024 * 1024, collective_id=0, has_side_effects=True),
        name="attention",
    )(queries, grad_out, keys, values, mask)


def window_mask(segments, index, rows):
    padding = DEPTH * rows
    base = index * rows
    seg_pad = jnp.concatenate([jnp.full((padding,), -1, jnp.int32), segments])
    seg_query = lax.dynamic_slice_in_dim(segments, base, rows, 0)
    seg_keys = lax.dynamic_slice_in_dim(seg_pad, base, SPAN * rows, 0)
    query_pos = jnp.arange(rows, dtype=jnp.int32)
    key_pos = jnp.arange(SPAN * rows, dtype=jnp.int32) - padding
    allowed = (seg_keys[:, None] == seg_query[None, :]) & (key_pos[:, None] <= query_pos[None, :])
    return jnp.where(allowed, 0.0, MASKED).astype(jnp.bfloat16)


def body(queries, keys, values, grad_out, segments):
    mask = window_mask(segments, lax.axis_index("dp"), queries.shape[0])
    return tuple(attention(lax.axis_size("dp"), queries, grad_out, keys, values, mask))


def solution(mesh):
    placed = (P("dp", "head"), P("dp", "head"), P("dp", "head"), P(("dp", "head"), None), P())
    return jax.shard_map(
        body,
        mesh=mesh,
        in_specs=placed,
        out_specs=(P(("dp", "head"), None), P("dp", "head"), P("dp", "head"), P("dp", "head")),
        check_vma=False,
    )
```

```python
import functools
import math

import jax
import jax.numpy as jnp
from jax import lax
from jax.experimental import pallas as pl
from jax.experimental.pallas import tpu as pltpu
from jax.sharding import PartitionSpec as P

QHEADS = 96
KVHEADS = 8
HEAD_DIM = 128
DEPTH = 8
SPAN = DEPTH + 1
RING = DEPTH // 2
GROUP = QHEADS // KVHEADS
MASKED = -(2.0**100)
SCALE = 1.0 / math.sqrt(HEAD_DIM)
NT = (((1,), (1,)), ((), ()))


def dot(a, b):
    return jnp.dot(a, b, preferred_element_type=jnp.float32)


def dot_nt(a, b):
    return lax.dot_general(a, b, NT, preferred_element_type=jnp.float32)


def attend_group(q_at, g_at, k_at, v_at, put_out, put_dq, put_dk, put_dv, tmp):
    (k_aug, v_aug, k_t, v_t, q_aug, g_aug, q_norm, g_norm, p_all, ds_all) = tmp[:10]
    scores, slopes = tmp[10:12], tmp[12:14]
    rows = HEAD_DIM
    for j in range(SPAN):
        at = pl.ds(j * rows, rows)
        k_j, v_j = k_at(j), v_at(j)
        k_aug[at, :HEAD_DIM] = k_j
        v_aug[at, :HEAD_DIM] = v_j
        k_t[:, j * rows : (j + 1) * rows] = k_j.T
        v_t[:HEAD_DIM, j * rows : (j + 1) * rows] = v_j.T
    for h in range(GROUP):
        spot = (h // 4, pl.ds(h % 4 * rows, rows), slice(0, HEAD_DIM))
        q_aug[spot] = q_at(h)
        g_aug[spot] = g_at(h)

    two = 2 * rows
    lane = lax.broadcasted_iota(jnp.int32, (two, HEAD_DIM), 1)

    def quad_step(i, carry):
        at = [slice(t * two, (t + 1) * two) for t in range(2)]
        inv_t = [None, None]

        def softmax(t):
            score = scores[t]
            top = score[0:rows, :].reshape(rows // 8, 8, two).max(axis=0)
            for j in range(1, SPAN):
                part = score[j * rows : (j + 1) * rows, :]
                top = jnp.maximum(top, part.reshape(rows // 8, 8, two).max(axis=0))
            top = jnp.max(top, axis=0, keepdims=True)
            for j in range(SPAN):
                part = score[j * rows : (j + 1) * rows, :]
                e = jnp.exp2((part - top) * (SCALE * math.log2(math.e)))
                p_all[i, j * rows : (j + 1) * rows, at[t]] = e.astype(jnp.bfloat16)

        def output(t):
            both = dot(v_t[...], p_all[i, :, at[t]])
            inv = 1.0 / both[HEAD_DIM : HEAD_DIM + 1]
            inv_t[t] = jnp.broadcast_to(inv, (HEAD_DIM, two)).T
            out = (both[:HEAD_DIM].T * inv_t[t]).astype(jnp.bfloat16)
            put_out(4 * i + 2 * t, out[:rows])
            put_out(4 * i + 2 * t + 1, out[rows:])
            g_pair = g_aug[i, at[t], :HEAD_DIM].astype(jnp.float32)
            delta = -jnp.sum(g_pair * out.astype(jnp.float32), axis=1, keepdims=True)
            hi = delta.astype(jnp.bfloat16).astype(jnp.float32)
            mid = (delta - hi).astype(jnp.bfloat16).astype(jnp.float32)
            low = delta - hi - mid
            tail = jnp.where(lane == 0, hi, jnp.where(lane == 1, mid, jnp.where(lane == 2, low, 0.0)))
            g_aug[i, at[t], HEAD_DIM:] = tail.astype(jnp.bfloat16)
            q_pair = q_aug[i, at[t], :HEAD_DIM].astype(jnp.float32)
            q_norm[i, at[t], :] = (q_pair * inv_t[t]).astype(jnp.bfloat16)
            g_norm[i, at[t], :] = (g_pair * inv_t[t]).astype(jnp.bfloat16)

        def grad_weights(t):
            slopes[t][...] = dot_nt(v_aug[...], g_aug[i, at[t], :])

        def grad_scores(t):
            for j in range(SPAN):
                keys = slice(j * rows, (j + 1) * rows)
                slope = slopes[t][keys, :].astype(jnp.bfloat16)
                ds_all[i, keys, at[t]] = p_all[i, keys, at[t]] * slope

        def grad_query(t):
            dq = (dot(k_t[...], ds_all[i, :, at[t]]).T * (inv_t[t] * SCALE)).astype(jnp.bfloat16)
            put_dq(4 * i + 2 * t, dq[:rows])
            put_dq(4 * i + 2 * t + 1, dq[rows:])

        scores[0][...] = dot_nt(k_aug[...], q_aug[i, at[0], :])
        softmax(0)
        scores[1][...] = dot_nt(k_aug[...], q_aug[i, at[1], :])
        output(0)
        softmax(1)
        grad_weights(0)
        output(1)
        grad_scores(0)
        grad_weights(1)
        grad_query(0)
        grad_scores(1)
        grad_query(1)
        return carry

    lax.fori_loop(0, GROUP // 4, quad_step, 0)
    for j in range(0, SPAN, 3):
        keys = slice(j * rows, (j + 3) * rows)
        dk = sum(dot(ds_all[i, keys, :], q_norm[i]) for i in range(GROUP // 4))
        dv = sum(dot(p_all[i, keys, :], g_norm[i]) for i in range(GROUP // 4))
        for b in range(3):
            put_dk(j + b, (SCALE * dk[b * rows : (b + 1) * rows]).astype(jnp.bfloat16))
            put_dv(j + b, dv[b * rows : (b + 1) * rows].astype(jnp.bfloat16))


def block_mask(seg_ref, me, j):
    rows = seg_ref.shape[1]
    key_block = me - DEPTH + j
    square = (rows, rows)
    key_seg = jnp.broadcast_to(seg_ref[pl.ds(jnp.maximum(key_block, 0), 1), :], square).T
    query_seg = jnp.broadcast_to(seg_ref[pl.ds(me, 1), :], square)
    behind = lax.broadcasted_iota(jnp.int32, square, 0) - lax.broadcasted_iota(jnp.int32, square, 1)
    allowed = (key_seg == query_seg) & (behind <= rows * (DEPTH - j))
    return jnp.where(allowed & (key_block >= 0), 0.0, MASKED).astype(jnp.bfloat16)


def fill_constants(seg_ref, me, tmp):
    k_aug, v_aug, v_t, q_aug = tmp[0], tmp[1], tmp[3], tmp[4]
    v_t[HEAD_DIM:, :] = jnp.ones((v_t.shape[0] - HEAD_DIM, v_t.shape[1]), jnp.bfloat16)
    for j in range(SPAN):
        k_aug[j * HEAD_DIM : (j + 1) * HEAD_DIM, HEAD_DIM:] = block_mask(seg_ref, me, j)
    ones = lax.broadcasted_iota(jnp.int32, (v_aug.shape[0], HEAD_DIM), 1) < 3
    v_aug[:, HEAD_DIM:] = jnp.where(ones, 1.0, 0.0).astype(jnp.bfloat16)
    side = (HEAD_DIM, HEAD_DIM)
    eye = lax.broadcasted_iota(jnp.int32, side, 0) == lax.broadcasted_iota(jnp.int32, side, 1)
    for h in range(GROUP):
        spot = (h // 4, pl.ds(h % 4 * HEAD_DIM, HEAD_DIM), slice(HEAD_DIM, None))
        q_aug[spot] = jnp.where(eye, 1.0, 0.0).astype(jnp.bfloat16)


def scratch(rows):
    window, quads, four = SPAN * rows, GROUP // 4, 4 * rows
    return [
        pltpu.VMEM((window, 2 * HEAD_DIM), jnp.bfloat16),
        pltpu.VMEM((window, 2 * HEAD_DIM), jnp.bfloat16),
        pltpu.VMEM((HEAD_DIM, window), jnp.bfloat16),
        pltpu.VMEM((HEAD_DIM + 16, window), jnp.bfloat16),
        pltpu.VMEM((quads, four, 2 * HEAD_DIM), jnp.bfloat16),
        pltpu.VMEM((quads, four, 2 * HEAD_DIM), jnp.bfloat16),
        pltpu.VMEM((quads, four, HEAD_DIM), jnp.bfloat16),
        pltpu.VMEM((quads, four, HEAD_DIM), jnp.bfloat16),
        pltpu.VMEM((quads, window, four), jnp.bfloat16),
        pltpu.VMEM((quads, window, four), jnp.bfloat16),
    ] + [pltpu.VMEM((window, 2 * rows), jnp.float32)] * 4


MESH = pl.DeviceIdType.MESH


def kernel(count, q_ref, grad_ref, key_ref, value_ref, seg_ref, out_ref, dq_ref, dk_ref, dv_ref,
           window, partial, first_in, second_in, far_out, far_in, near_out, near_in, total,
           g_heads, o_heads, o_arrived,
           kv_send, kv_recv, first_send, first_recv, second_send, second_recv,
           far_send, far_recv, near_send, near_recv, g_send, g_recv, o_send, o_recv, *tmp):
    me, core = lax.axis_index("dp"), lax.axis_index("head")
    spot = lax.rem(me, RING)
    heads = window.shape[0]
    half, columns = grad_ref.shape[0], q_ref.shape[1]
    width = GROUP * HEAD_DIM
    below, above = me >= RING, me + RING < count
    two_below = me >= 2 * RING

    def lanes(start, size):
        return pl.ds(pl.multiple_of(start, HEAD_DIM), size)

    mine, other = core * columns, (1 - core) * columns
    my_rows = pl.ds(pl.multiple_of(core * half, half), half)
    other_rows = pl.ds(pl.multiple_of((1 - core) * half, half), half)

    def remote(source, target, send, recv, place, side=None):
        return pltpu.make_async_remote_copy(
            source, target, send, recv,
            device_id=(place, core if side is None else side), device_id_type=MESH)

    up = lax.rem(me + RING, count)
    down = lax.rem(me - RING + count, count)

    def peer(k):
        return me - spot + lax.rem(spot + k, RING)

    def step_to(k):
        return lax.rem(spot + k, RING) - spot

    def near_kv(h):
        return remote(window.at[h, DEPTH], window.at[h, RING], kv_send.at[h, 0], kv_recv.at[h, RING], up)

    def far_kv(h):
        return remote(window.at[h, RING], window.at[h, 0], kv_send.at[h, 1], kv_recv.at[h, 0], up)

    def ring_kv(h, k, held, slot):
        which = 1 + k if held == RING else 4 + k
        return remote(window.at[h, held], window.at[h, slot], kv_send.at[h, which], kv_recv.at[h, slot], peer(k))

    def arrival(h, slot):
        return remote(window.at[h, slot], window.at[h, slot], kv_send.at[h, 0], kv_recv.at[h, slot], up)

    def first_copy(h, k):
        return remote(partial.at[h, RING + step_to(k)], first_in.at[h, k - 1],
                      first_send.at[h, k - 1], first_recv.at[h, k - 1], peer(k))

    def second_copy(h, k):
        slot = jnp.where(step_to(k) > 0, step_to(k), DEPTH + step_to(k))
        return remote(partial.at[h, slot], second_in.at[h, k - 1],
                      second_send.at[h, k - 1], second_recv.at[h, k - 1], peer(k))

    def far_copy(h):
        return remote(far_out.at[h], far_in.at[h], far_send.at[h], far_recv.at[h], down)

    def near_copy(h):
        return remote(near_out.at[h], near_in.at[h], near_send.at[h], near_recv.at[h], down)

    def g_copy(h):
        return remote(grad_ref.at[:, lanes(other + h * width, width)],
                      g_heads.at[my_rows, lanes(h * width, width)], g_send.at[h], g_recv.at[h], me, 1 - core)

    def o_copy(h):
        return remote(o_heads.at[other_rows, lanes(h * width, width)],
                      o_arrived.at[:, lanes(h * width, width)], o_send.at[h], o_recv.at[h], me, 1 - core)

    def greet(place, side):
        pl.semaphore_signal(barrier, inc=1, device_id=(place, side), device_id_type=MESH)

    barrier = pltpu.get_barrier_semaphore()
    greet(me, 1 - core)
    for k in range(1, RING):
        greet(peer(k), core)
    pl.when(above)(lambda: greet(up, core))
    pl.when(below)(lambda: greet(down, core))

    for h in range(heads):
        window[h, DEPTH, 0] = key_ref[:, h * HEAD_DIM : (h + 1) * HEAD_DIM]
        window[h, DEPTH, 1] = value_ref[:, h * HEAD_DIM : (h + 1) * HEAD_DIM]
    for d in range(1, SPAN):
        @pl.when(me < d)
        def _():
            window[:, DEPTH - d] = jnp.zeros((heads,) + window.shape[2:], jnp.bfloat16)

    pl.semaphore_wait(barrier, RING + jnp.where(below, 1, 0) + jnp.where(above, 1, 0))

    def send_out(h, carry):
        pl.when(above)(lambda: near_kv(h).start())
        g_copy(h).start()
        return carry

    def send_own(h, wait=False):
        for k in range(1, RING):
            @pl.when(step_to(k) > 0)
            def _():
                copy = ring_kv(h, k, DEPTH, DEPTH - step_to(k))
                copy.wait_send() if wait else copy.start()

    def send_near(h, wait=False):
        @pl.when(below)
        def _():
            for k in range(1, RING):
                copy = ring_kv(h, k, RING, RING - step_to(k))
                copy.wait_send() if wait else copy.start()

    def send_far(h, wait=False):
        @pl.when(two_below)
        def _():
            if not wait:
                arrival(h, 0).wait_recv()
            for k in range(1, RING):
                @pl.when(step_to(k) < 0)
                def _():
                    copy = ring_kv(h, k, 0, -step_to(k))
                    copy.wait_send() if wait else copy.start()

    def relay(h, carry):
        @pl.when(below)
        def _():
            arrival(h, RING).wait_recv()
            pl.when(above)(lambda: far_kv(h).start())
        return carry

    def spread(h):
        send_own(h)
        send_near(h)
        send_far(h)

    lax.fori_loop(0, heads, send_out, 0)
    g_heads[my_rows, :] = grad_ref[:, lanes(mine, columns)]
    fill_constants(seg_ref, me, tmp)
    lax.fori_loop(0, heads, relay, 0)
    spread(0)

    def merge_far(h):
        @pl.when(two_below)
        def _():
            total[...] = partial[h, 0].astype(jnp.float32)
            for k in range(1, RING):
                @pl.when(spot >= k)
                def _():
                    second_copy(h, k).wait_recv()
                    total[...] += second_in[h, k - 1].astype(jnp.float32)
            far_out[h] = total[...].astype(jnp.bfloat16)
            far_copy(h).start()

    def merge_near(h):
        @pl.when(below)
        def _():
            total[...] = partial[h, RING].astype(jnp.float32)
            for k in range(1, RING):
                first_copy(h, k).wait_recv()
                total[...] += first_in[h, k - 1].astype(jnp.float32)

            @pl.when(above)
            def _():
                far_copy(h).wait_recv()
                total[...] += far_in[h].astype(jnp.float32)
            near_out[h] = total[...].astype(jnp.bfloat16)
            near_copy(h).start()

    def head_step(h, carry):
        pl.when(h + 1 < heads)(lambda: spread(h + 1))
        g_copy(h).wait_recv()
        for d in range(1, SPAN):
            if d % RING:
                @pl.when(me >= d)
                def _():
                    arrival(h, DEPTH - d).wait_recv()

        def at(ref, g):
            return ref[:, lanes(h * width + g * HEAD_DIM, HEAD_DIM)]

        def put(ref, g, value):
            ref[:, lanes(h * width + g * HEAD_DIM, HEAD_DIM)] = value

        def put_block(which, j, value):
            partial[h, j, which] = value

        attend_group(
            functools.partial(at, q_ref),
            functools.partial(at, g_heads),
            lambda j: window[h, j, 0],
            lambda j: window[h, j, 1],
            functools.partial(put, o_heads),
            functools.partial(put, dq_ref),
            functools.partial(put_block, 0),
            functools.partial(put_block, 1),
            tmp,
        )
        for k in range(1, RING):
            pl.when(below)(lambda: first_copy(h, k).start())
            pl.when((step_to(k) < 0) | two_below)(lambda: second_copy(h, k).start())
        o_copy(h).start()
        out_ref[:, lanes(mine + h * width, width)] = o_heads[my_rows, lanes(h * width, width)]
        pl.when(h >= 1)(lambda: merge_far(h - 1))
        pl.when(h >= 2)(lambda: merge_near(h - 2))
        return carry

    lax.fori_loop(0, heads, head_step, 0)
    merge_far(heads - 1)
    if heads > 1:
        merge_near(heads - 2)
    merge_near(heads - 1)

    def finish_head(h, carry):
        total[...] = partial[h, DEPTH].astype(jnp.float32)
        for k in range(1, RING):
            @pl.when(spot < k)
            def _():
                second_copy(h, k).wait_recv()
                total[...] += second_in[h, k - 1].astype(jnp.float32)

        @pl.when(above)
        def _():
            near_copy(h).wait_recv()
            total[...] += near_in[h].astype(jnp.float32)
        dk_ref[:, lanes(h * HEAD_DIM, HEAD_DIM)] = total[0].astype(jnp.bfloat16)
        dv_ref[:, lanes(h * HEAD_DIM, HEAD_DIM)] = total[1].astype(jnp.bfloat16)

        g_copy(h).wait_send()
        o_copy(h).wait()
        send_own(h, wait=True)
        send_near(h, wait=True)
        send_far(h, wait=True)
        for k in range(1, RING):
            pl.when(below)(lambda: first_copy(h, k).wait_send())
            pl.when((step_to(k) < 0) | two_below)(lambda: second_copy(h, k).wait_send())
        pl.when(above)(lambda: near_kv(h).wait_send())
        pl.when(above & below)(lambda: far_kv(h).wait_send())
        pl.when(below)(lambda: near_copy(h).wait_send())
        pl.when(two_below)(lambda: far_copy(h).wait_send())
        return carry

    lax.fori_loop(0, heads, finish_head, 0)
    out_ref[:, lanes(other, columns)] = o_arrived[...]


def attention(count, queries, grad_out, keys, values, segments):
    rows, columns = queries.shape
    heads = keys.shape[1] // HEAD_DIM
    half = grad_out.shape[0]
    tile = (2, rows, HEAD_DIM)
    in_vmem = pl.BlockSpec(memory_space=pltpu.VMEM)
    blocks = [(SPAN,), (SPAN,), (RING - 1,), (RING - 1,), (), (), (), ()]
    counts = [DEPTH, SPAN] + [RING - 1] * 4
    return pl.pallas_call(
        functools.partial(kernel, count),
        in_specs=[in_vmem] * 5,
        out_specs=[in_vmem] * 4,
        out_shape=[jax.ShapeDtypeStruct(a.shape, jnp.bfloat16) for a in (grad_out, queries, keys, values)],
        scratch_shapes=[pltpu.VMEM((heads,) + b + tile, jnp.bfloat16) for b in blocks]
        + [
            pltpu.VMEM(tile, jnp.float32),
            pltpu.VMEM((rows, columns), jnp.bfloat16),
            pltpu.VMEM((rows, columns), jnp.bfloat16),
            pltpu.VMEM((half, columns), jnp.bfloat16),
        ]
        + [pltpu.SemaphoreType.DMA((heads, n)) for n in counts]
        + [pltpu.SemaphoreType.DMA((heads,))] * 8
        + scratch(rows),
        compiler_params=pltpu.CompilerParams(
            vmem_limit_bytes=56 * 1024 * 1024, collective_id=0, has_side_effects=True),
        name="attention",
    )(queries, grad_out, keys, values, segments)


def body(queries, keys, values, grad_out, segments):
    by_block = segments.reshape(-1, queries.shape[0])
    return tuple(attention(lax.axis_size("dp"), queries, grad_out, keys, values, by_block))


def solution(mesh):
    placed = (P("dp", "head"), P("dp", "head"), P("dp", "head"), P(("dp", "head"), None), P())
    return jax.shard_map(
        body,
        mesh=mesh,
        in_specs=placed,
        out_specs=(P(("dp", "head"), None), P("dp", "head"), P("dp", "head"), P("dp", "head")),
        check_vma=False,
    )
```

```python
import functools
import math

import jax
import jax.numpy as jnp
from jax import lax
from jax.experimental import pallas as pl
from jax.experimental.pallas import tpu as pltpu
from jax.sharding import PartitionSpec as P

QHEADS = 96
KVHEADS = 8
HEAD_DIM = 128
DEPTH = 8
SPAN = DEPTH + 1
RING = DEPTH // 2
GROUP = QHEADS // KVHEADS
PAIRS = GROUP // 2
MASKED = -(2.0**100)
SCALE = 1.0 / math.sqrt(HEAD_DIM)
NT = (((1,), (1,)), ((), ()))


def dot(a, b):
    return jnp.dot(a, b, preferred_element_type=jnp.float32)


def dot_nt(a, b):
    return lax.dot_general(a, b, NT, preferred_element_type=jnp.float32)


def attend_group(q_at, g_at, k_at, v_at, put_out, put_dq, put_dk, put_dv, stored, tmp):
    (k_aug, v_aug, k_t, v_t, q_aug, g_aug, q_norm, g_norm, p_all, ds_all) = tmp[:10]
    scores, slopes = tmp[10:12], tmp[12:14]
    rows = HEAD_DIM
    for j in range(SPAN):
        at = pl.ds(j * rows, rows)
        k_j, v_j = k_at(j), v_at(j)
        k_aug[at, :HEAD_DIM] = k_j
        v_aug[at, :HEAD_DIM] = v_j
        k_t[:, j * rows : (j + 1) * rows] = k_j.T
        v_t[:HEAD_DIM, j * rows : (j + 1) * rows] = v_j.T
    for h in range(GROUP):
        spot = (h // 4, pl.ds(h % 4 * rows, rows), slice(0, HEAD_DIM))
        q_aug[spot] = q_at(h)
        g_aug[spot] = g_at(h)

    two = 2 * rows
    lane = lax.broadcasted_iota(jnp.int32, (two, HEAD_DIM), 1)

    def place(t):
        return t // 2, slice(t % 2 * two, (t % 2 + 1) * two)

    inv_t = [None] * PAIRS

    def softmax(t):
        i, at = place(t)
        score = scores[t % 2]
        top = score[0:rows, :].reshape(rows // 8, 8, two).max(axis=0)
        for j in range(1, SPAN):
            part = score[j * rows : (j + 1) * rows, :]
            top = jnp.maximum(top, part.reshape(rows // 8, 8, two).max(axis=0))
        top = jnp.max(top, axis=0, keepdims=True)
        for j in range(SPAN):
            part = score[j * rows : (j + 1) * rows, :]
            e = jnp.exp2((part - top) * (SCALE * math.log2(math.e)))
            p_all[i, j * rows : (j + 1) * rows, at] = e.astype(jnp.bfloat16)

    def output(t):
        i, at = place(t)
        both = dot(v_t[...], p_all[i, :, at])
        inv = 1.0 / both[HEAD_DIM : HEAD_DIM + 1]
        inv_t[t] = jnp.broadcast_to(inv, (HEAD_DIM, two)).T
        out = (both[:HEAD_DIM].T * inv_t[t]).astype(jnp.bfloat16)
        put_out(2 * t, out[:rows])
        put_out(2 * t + 1, out[rows:])
        g_pair = g_aug[i, at, :HEAD_DIM].astype(jnp.float32)
        delta = -jnp.sum(g_pair * out.astype(jnp.float32), axis=1, keepdims=True)
        hi = delta.astype(jnp.bfloat16).astype(jnp.float32)
        mid = (delta - hi).astype(jnp.bfloat16).astype(jnp.float32)
        low = delta - hi - mid
        tail = jnp.where(lane == 0, hi, jnp.where(lane == 1, mid, jnp.where(lane == 2, low, 0.0)))
        g_aug[i, at, HEAD_DIM:] = tail.astype(jnp.bfloat16)
        q_pair = q_aug[i, at, :HEAD_DIM].astype(jnp.float32)
        q_norm[i, at, :] = (q_pair * inv_t[t]).astype(jnp.bfloat16)
        g_norm[i, at, :] = (g_pair * inv_t[t]).astype(jnp.bfloat16)

    def grad_weights(t):
        i, at = place(t)
        slopes[t % 2][...] = dot_nt(v_aug[...], g_aug[i, at, :])

    def grad_scores(t):
        i, at = place(t)
        for j in range(SPAN):
            keys = slice(j * rows, (j + 1) * rows)
            slope = slopes[t % 2][keys, :].astype(jnp.bfloat16)
            ds_all[i, keys, at] = p_all[i, keys, at] * slope

    def grad_query(t):
        i, at = place(t)
        dq = (dot(k_t[...], ds_all[i, :, at]).T * (inv_t[t] * SCALE)).astype(jnp.bfloat16)
        put_dq(2 * t, dq[:rows])
        put_dq(2 * t + 1, dq[rows:])

    def raw_scores(t):
        i, at = place(t)
        scores[t % 2][...] = dot_nt(k_aug[...], q_aug[i, at, :])

    raw_scores(0)
    for t in range(PAIRS):
        if t + 1 < PAIRS:
            raw_scores(t + 1)
        softmax(t)
        if t > 0:
            grad_scores(t - 1)
        output(t)
        grad_weights(t)
        if t > 0:
            grad_query(t - 1)
    grad_scores(PAIRS - 1)
    grad_query(PAIRS - 1)
    for j in range(0, SPAN, 3):
        keys = slice(j * rows, (j + 3) * rows)
        dk = sum(dot(ds_all[i, keys, :], q_norm[i]) for i in range(GROUP // 4))
        dv = sum(dot(p_all[i, keys, :], g_norm[i]) for i in range(GROUP // 4))
        for b in range(3):
            put_dk(j + b, (SCALE * dk[b * rows : (b + 1) * rows]).astype(jnp.bfloat16))
            put_dv(j + b, dv[b * rows : (b + 1) * rows].astype(jnp.bfloat16))
        stored(j, j + 3)


def block_mask(seg_ref, me, j):
    rows = seg_ref.shape[1]
    key_block = me - DEPTH + j
    square = (rows, rows)
    key_seg = jnp.broadcast_to(seg_ref[pl.ds(jnp.maximum(key_block, 0), 1), :], square).T
    query_seg = jnp.broadcast_to(seg_ref[pl.ds(me, 1), :], square)
    behind = lax.broadcasted_iota(jnp.int32, square, 0) - lax.broadcasted_iota(jnp.int32, square, 1)
    allowed = (key_seg == query_seg) & (behind <= rows * (DEPTH - j))
    return jnp.where(allowed & (key_block >= 0), 0.0, MASKED).astype(jnp.bfloat16)


def fill_constants(seg_ref, me, tmp):
    k_aug, v_aug, v_t, q_aug = tmp[0], tmp[1], tmp[3], tmp[4]
    v_t[HEAD_DIM:, :] = jnp.ones((v_t.shape[0] - HEAD_DIM, v_t.shape[1]), jnp.bfloat16)
    for j in range(SPAN):
        k_aug[j * HEAD_DIM : (j + 1) * HEAD_DIM, HEAD_DIM:] = block_mask(seg_ref, me, j)
    ones = lax.broadcasted_iota(jnp.int32, (v_aug.shape[0], HEAD_DIM), 1) < 3
    v_aug[:, HEAD_DIM:] = jnp.where(ones, 1.0, 0.0).astype(jnp.bfloat16)
    side = (HEAD_DIM, HEAD_DIM)
    eye = lax.broadcasted_iota(jnp.int32, side, 0) == lax.broadcasted_iota(jnp.int32, side, 1)
    for h in range(GROUP):
        spot = (h // 4, pl.ds(h % 4 * HEAD_DIM, HEAD_DIM), slice(HEAD_DIM, None))
        q_aug[spot] = jnp.where(eye, 1.0, 0.0).astype(jnp.bfloat16)


def scratch(rows):
    window, quads, four = SPAN * rows, GROUP // 4, 4 * rows
    return [
        pltpu.VMEM((window, 2 * HEAD_DIM), jnp.bfloat16),
        pltpu.VMEM((window, 2 * HEAD_DIM), jnp.bfloat16),
        pltpu.VMEM((HEAD_DIM, window), jnp.bfloat16),
        pltpu.VMEM((HEAD_DIM + 16, window), jnp.bfloat16),
        pltpu.VMEM((quads, four, 2 * HEAD_DIM), jnp.bfloat16),
        pltpu.VMEM((quads, four, 2 * HEAD_DIM), jnp.bfloat16),
        pltpu.VMEM((quads, four, HEAD_DIM), jnp.bfloat16),
        pltpu.VMEM((quads, four, HEAD_DIM), jnp.bfloat16),
        pltpu.VMEM((quads, window, four), jnp.bfloat16),
        pltpu.VMEM((quads, window, four), jnp.bfloat16),
    ] + [pltpu.VMEM((window, 2 * rows), jnp.float32)] * 4


MESH = pl.DeviceIdType.MESH


def kernel(count, q_ref, grad_ref, key_ref, value_ref, seg_ref, out_ref, dq_ref, dk_ref, dv_ref,
           window, partial, first_in, second_in, far_out, far_in, near_out, near_in, total,
           q_heads, g_heads, o_heads, dq_heads,
           kv_send, kv_recv, first_send, first_recv, second_send, second_recv,
           far_send, far_recv, near_send, near_recv, g_send, g_recv, o_send, o_recv,
           own_sem, dq_sem, in_sem, *tmp):
    me, core = lax.axis_index("dp"), lax.axis_index("head")
    spot = lax.rem(me, RING)
    heads = window.shape[0]
    half, columns = grad_ref.shape[0], q_ref.shape[1]
    width = GROUP * HEAD_DIM
    below, above = me >= RING, me + RING < count
    two_below = me >= 2 * RING

    def lanes(start, size):
        return pl.ds(pl.multiple_of(start, HEAD_DIM), size)

    mine, other = core * columns, (1 - core) * columns
    my_rows = pl.ds(pl.multiple_of(core * half, half), half)
    other_rows = pl.ds(pl.multiple_of((1 - core) * half, half), half)

    def remote(source, target, send, recv, place, side=None):
        return pltpu.make_async_remote_copy(
            source, target, send, recv,
            device_id=(place, core if side is None else side), device_id_type=MESH)

    up = lax.rem(me + RING, count)
    down = lax.rem(me - RING + count, count)

    def peer(k):
        return me - spot + lax.rem(spot + k, RING)

    def step_to(k):
        return lax.rem(spot + k, RING) - spot

    def near_kv(h):
        return remote(window.at[h, DEPTH], window.at[h, RING], kv_send.at[h, 0], kv_recv.at[h, RING], up)

    def far_kv(h):
        return remote(window.at[h, RING], window.at[h, 0], kv_send.at[h, 1], kv_recv.at[h, 0], up)

    def ring_kv(h, k, held, slot):
        which = 1 + k if held == RING else 4 + k
        return remote(window.at[h, held], window.at[h, slot], kv_send.at[h, which], kv_recv.at[h, slot], peer(k))

    def arrival(h, slot):
        return remote(window.at[h, slot], window.at[h, slot], kv_send.at[h, 0], kv_recv.at[h, slot], up)

    def first_copy(h, k):
        return remote(partial.at[h, RING + step_to(k)], first_in.at[h, k - 1],
                      first_send.at[h, k - 1], first_recv.at[h, k - 1], peer(k))

    def second_copy(h, k):
        slot = jnp.where(step_to(k) > 0, step_to(k), DEPTH + step_to(k))
        return remote(partial.at[h, slot], second_in.at[h, k - 1],
                      second_send.at[h, k - 1], second_recv.at[h, k - 1], peer(k))

    def far_copy(h):
        return remote(far_out.at[h], far_in.at[h], far_send.at[h], far_recv.at[h], down)

    def near_copy(h):
        return remote(near_out.at[h], near_in.at[h], near_send.at[h], near_recv.at[h], down)

    def g_copy(h):
        return remote(grad_ref.at[:, lanes(other + h * width, width)],
                      g_heads.at[my_rows, lanes(h * width, width)], g_send.at[h], g_recv.at[h], me, 1 - core)

    def o_copy(h):
        return remote(o_heads.at[other_rows, lanes(h * width, width)],
                      out_ref.at[:, lanes(mine + h * width, width)], o_send.at[h], o_recv.at[h], me, 1 - core)

    def own_out(h):
        return pltpu.make_async_copy(o_heads.at[my_rows, lanes(h * width, width)],
                                     out_ref.at[:, lanes(mine + h * width, width)], own_sem.at[h])

    def dq_out(h):
        part = (slice(None), lanes(h * width, width))
        return pltpu.make_async_copy(dq_heads.at[part], dq_ref.at[part], dq_sem.at[h])

    q_in = pltpu.make_async_copy(q_ref, q_heads, in_sem.at[0])
    g_in = pltpu.make_async_copy(grad_ref.at[:, lanes(mine, columns)], g_heads.at[my_rows, :], in_sem.at[1])

    def greet(place, side):
        pl.semaphore_signal(barrier, inc=1, device_id=(place, side), device_id_type=MESH)

    g_in.start()
    q_in.start()
    barrier = pltpu.get_barrier_semaphore()
    greet(me, 1 - core)
    for k in range(1, RING):
        greet(peer(k), core)
    pl.when(above)(lambda: greet(up, core))
    pl.when(below)(lambda: greet(down, core))

    for h in range(heads):
        window[h, DEPTH, 0] = key_ref[:, h * HEAD_DIM : (h + 1) * HEAD_DIM]
        window[h, DEPTH, 1] = value_ref[:, h * HEAD_DIM : (h + 1) * HEAD_DIM]
    for d in range(1, SPAN):
        @pl.when(me < d)
        def _():
            window[:, DEPTH - d] = jnp.zeros((heads,) + window.shape[2:], jnp.bfloat16)

    pl.semaphore_wait(barrier, RING + jnp.where(below, 1, 0) + jnp.where(above, 1, 0))

    def send_out(h, carry):
        pl.when(above)(lambda: near_kv(h).start())
        g_copy(h).start()
        return carry

    def send_own(h, wait=False):
        for k in range(1, RING):
            @pl.when(step_to(k) > 0)
            def _():
                copy = ring_kv(h, k, DEPTH, DEPTH - step_to(k))
                copy.wait_send() if wait else copy.start()

    def send_near(h, wait=False):
        @pl.when(below)
        def _():
            for k in range(1, RING):
                copy = ring_kv(h, k, RING, RING - step_to(k))
                copy.wait_send() if wait else copy.start()

    def send_far(h, wait=False):
        @pl.when(two_below)
        def _():
            if not wait:
                arrival(h, 0).wait_recv()
            for k in range(1, RING):
                @pl.when(step_to(k) < 0)
                def _():
                    copy = ring_kv(h, k, 0, -step_to(k))
                    copy.wait_send() if wait else copy.start()

    def relay(h, carry):
        @pl.when(below)
        def _():
            arrival(h, RING).wait_recv()
            pl.when(above)(lambda: far_kv(h).start())
        return carry

    def spread(h):
        send_own(h)
        send_near(h)
        send_far(h)

    lax.fori_loop(0, heads, send_out, 0)
    fill_constants(seg_ref, me, tmp)
    lax.fori_loop(0, heads, relay, 0)
    spread(0)
    g_in.wait()
    q_in.wait()

    def merge_far(h):
        @pl.when(two_below)
        def _():
            total[...] = partial[h, 0].astype(jnp.float32)
            for k in range(1, RING):
                @pl.when(spot >= k)
                def _():
                    second_copy(h, k).wait_recv()
                    total[...] += second_in[h, k - 1].astype(jnp.float32)
            far_out[h] = total[...].astype(jnp.bfloat16)
            far_copy(h).start()

    def merge_near(h):
        @pl.when(below)
        def _():
            total[...] = partial[h, RING].astype(jnp.float32)
            for k in range(1, RING):
                first_copy(h, k).wait_recv()
                total[...] += first_in[h, k - 1].astype(jnp.float32)

            @pl.when(above)
            def _():
                far_copy(h).wait_recv()
                total[...] += far_in[h].astype(jnp.float32)
            near_out[h] = total[...].astype(jnp.bfloat16)
            near_copy(h).start()

    def head_step(h, carry):
        pl.when(h + 1 < heads)(lambda: spread(h + 1))
        g_copy(h).wait_recv()
        for d in range(1, SPAN):
            if d % RING:
                @pl.when(me >= d)
                def _():
                    arrival(h, DEPTH - d).wait_recv()

        def at(ref, g):
            return ref[:, lanes(h * width + g * HEAD_DIM, HEAD_DIM)]

        def put(ref, g, value):
            ref[:, lanes(h * width + g * HEAD_DIM, HEAD_DIM)] = value

        def put_block(which, j, value):
            partial[h, j, which] = value

        def send_slots(start, stop):
            for slot in range(start, stop):
                k = slot % RING
                if k == 0:
                    continue
                ahead = step_to(k) > 0
                if slot < RING:
                    pl.when(ahead & two_below)(lambda: second_copy(h, k).start())
                    pl.when(jnp.logical_not(ahead) & below)(lambda: first_copy(h, k).start())
                else:
                    pl.when(ahead & below)(lambda: first_copy(h, k).start())
                    pl.when(jnp.logical_not(ahead))(lambda: second_copy(h, k).start())

        attend_group(
            functools.partial(at, q_heads),
            functools.partial(at, g_heads),
            lambda j: window[h, j, 0],
            lambda j: window[h, j, 1],
            functools.partial(put, o_heads),
            functools.partial(put, dq_heads),
            functools.partial(put_block, 0),
            functools.partial(put_block, 1),
            send_slots,
            tmp,
        )
        o_copy(h).start()
        own_out(h).start()
        dq_out(h).start()
        pl.when(h >= 1)(lambda: merge_far(h - 1))
        pl.when(h >= 2)(lambda: merge_near(h - 2))
        return carry

    lax.fori_loop(0, heads, head_step, 0)

    def finish_head(h, carry):
        total[...] = partial[h, DEPTH].astype(jnp.float32)
        for k in range(1, RING):
            @pl.when(spot < k)
            def _():
                second_copy(h, k).wait_recv()
                total[...] += second_in[h, k - 1].astype(jnp.float32)

        @pl.when(above)
        def _():
            near_copy(h).wait_recv()
            total[...] += near_in[h].astype(jnp.float32)
        dk_ref[:, lanes(h * HEAD_DIM, HEAD_DIM)] = total[0].astype(jnp.bfloat16)
        dv_ref[:, lanes(h * HEAD_DIM, HEAD_DIM)] = total[1].astype(jnp.bfloat16)

        g_copy(h).wait_send()
        o_copy(h).wait_send()
        remote(o_heads.at[other_rows, lanes(h * width, width)],
               out_ref.at[:, lanes(other + h * width, width)],
               o_send.at[h], o_recv.at[h], me, 1 - core).wait_recv()
        own_out(h).wait()
        dq_out(h).wait()
        send_own(h, wait=True)
        send_near(h, wait=True)
        send_far(h, wait=True)
        for k in range(1, RING):
            pl.when(below)(lambda: first_copy(h, k).wait_send())
            pl.when((step_to(k) < 0) | two_below)(lambda: second_copy(h, k).wait_send())
        pl.when(above)(lambda: near_kv(h).wait_send())
        pl.when(above & below)(lambda: far_kv(h).wait_send())
        pl.when(below)(lambda: near_copy(h).wait_send())
        pl.when(two_below)(lambda: far_copy(h).wait_send())
        return carry

    early = max(heads - 2, 0)
    if heads > 1:
        merge_near(heads - 2)
    lax.fori_loop(0, early, finish_head, 0)
    merge_far(heads - 1)
    merge_near(heads - 1)
    lax.fori_loop(early, heads, finish_head, 0)


def attention(count, queries, grad_out, keys, values, segments):
    rows, columns = queries.shape
    heads = keys.shape[1] // HEAD_DIM
    tile = (2, rows, HEAD_DIM)
    in_vmem = pl.BlockSpec(memory_space=pltpu.VMEM)
    in_place = pl.BlockSpec(memory_space=pl.ANY)
    blocks = [(SPAN,), (SPAN,), (RING - 1,), (RING - 1,), (), (), (), ()]
    counts = [DEPTH, SPAN] + [RING - 1] * 4
    return pl.pallas_call(
        functools.partial(kernel, count),
        in_specs=[in_place] * 2 + [in_vmem] * 3,
        out_specs=[in_place] * 2 + [in_vmem] * 2,
        out_shape=[jax.ShapeDtypeStruct(a.shape, jnp.bfloat16) for a in (grad_out, queries, keys, values)],
        scratch_shapes=[pltpu.VMEM((heads,) + b + tile, jnp.bfloat16) for b in blocks]
        + [
            pltpu.VMEM(tile, jnp.float32),
        ]
        + [pltpu.VMEM((rows, columns), jnp.bfloat16)] * 4
        + [pltpu.SemaphoreType.DMA((heads, n)) for n in counts]
        + [pltpu.SemaphoreType.DMA((heads,))] * 10
        + [pltpu.SemaphoreType.DMA((2,))]
        + scratch(rows),
        compiler_params=pltpu.CompilerParams(
            vmem_limit_bytes=56 * 1024 * 1024, collective_id=0, has_side_effects=True),
        name="attention",
    )(queries, grad_out, keys, values, segments)


def body(queries, keys, values, grad_out, segments):
    by_block = segments.reshape(-1, queries.shape[0])
    return tuple(attention(lax.axis_size("dp"), queries, grad_out, keys, values, by_block))


def solution(mesh):
    placed = (P("dp", "head"), P("dp", "head"), P("dp", "head"), P(("dp", "head"), None), P())
    return jax.shard_map(
        body,
        mesh=mesh,
        in_specs=placed,
        out_specs=(P(("dp", "head"), None), P("dp", "head"), P("dp", "head"), P("dp", "head")),
        check_vma=False,
    )
```
